32 devices in a mesh: lat: 4 (over y, core), lon: 8 (over z, x).
Axes of the slice: x: 2, y: 2, z: 4, core: 2. Of those that a mesh axis runs over, the one named last changes fastest.
Arguments:
- cotangent: bfloat16 [4, 768, 32, 128], P('lat', 'lon'), may hold values from -6 to 6
- tiles: bfloat16 [64, 128, 128], replicated, may hold values from -0.25 to 0.25
- local_src: int32 [2, 4, 2304], P(None, 'lat', 'lon'), may hold values from 0 to 95
- local_tgt: int32 [2, 4, 2304], P(None, 'lat', 'lon'), may hold values from 0 to 95
- local_tile: int32 [2, 4, 2304], P(None, 'lat', 'lon'), may hold values from 0 to 63
- remote_src: int32 [2, 4, 2304], P(None, 'lat', 'lon'), may hold values from 0 to 95
- remote_tgt: int32 [2, 4, 2304], P(None, 'lat', 'lon'), may hold values from 0 to 95
- remote_tile: int32 [2, 4, 2304], P(None, 'lat', 'lon'), may hold values from 0 to 63
- remote_live: int32 [2, 4, 2304], P(None, 'lat', 'lon'), may hold values from 0 to 1, as said below
Outputs:
- initial_adjoint: float32 [4, 768, 32, 128], P('lat', 'lon')
The draws below stay inside these ranges and needn't reach their ends.
Inputs may be any that keep to these rules, and one draw needn't show every extreme that they name: `remote_live`: A device's remote slots are laid out by owner sector p, then band offset d of 0 to 2, then k < 12; in each (p, d) cell the live slots come first; on every device the cell of the next sector east with d = 1 is full; and on a device (a, b) with 0 < a < 7, every cell whose owner sector p lies more than 4 sectors from b (counting around the circle) is empty.
All inputs are finite; a program needn't handle non-finite values.
Results may differ from the reference program's by a relative error of at most 0.0029.
Values may be sent and summed in bfloat16 or wider, within the bound.
A program may use at most 192 MiB of HBM per device.

```python
import math
import jax
import jax.numpy as jnp
from jax import lax

CH = 32
PTS = 128
NTILES = 64
BLK_DEV = 96
CAP = 12
STEPS = 2
LOC = 288
SLOTS = 288
N_LAT = 4
N_LON = 8


def draw_remote_live(key, part):
    cell_shape = (STEPS, N_LAT, N_LON, N_LON, 3)
    band_index = lax.broadcasted_iota(jnp.int32, cell_shape, 1)
    sector = lax.broadcasted_iota(jnp.int32, cell_shape, 2)
    owner_sector = lax.broadcasted_iota(jnp.int32, cell_shape, 3)
    offset = lax.broadcasted_iota(jnp.int32, cell_shape, 4)
    counts = jax.random.randint(key, cell_shape, CAP // 2, CAP + 1)
    polar = (band_index == 0) | (band_index == N_LAT - 1)
    across = (band_index == 0) & (offset == 0) | (band_index == N_LAT - 1) & (offset == 2)
    center = jnp.where(across, (sector + N_LON // 2) % N_LON, sector)
    distance = jnp.abs(owner_sector - center)
    distance = jnp.minimum(distance, N_LON - distance)
    reach = jnp.where(polar, N_LON // 2, N_LON // 4)
    counts = jnp.where(distance <= reach, counts, 0)
    forced = (owner_sector == (sector + 1) % N_LON) & (offset == 1)
    counts = jnp.where(forced, CAP, counts)
    slot_index = jnp.arange(CAP, dtype=jnp.int32)
    live = (slot_index[None, None, None, None, None, :] < counts[..., None]).astype(jnp.int32)
    return live.reshape(STEPS, N_LAT, N_LON * N_LON * 3 * CAP)


def with_ends(entries, key, smallest, high):
    index_at = [jax.random.randint(jax.random.fold_in(key, axis), (), 0, length) for axis, length in enumerate(entries.shape)]
    main_axis = entries.shape.index(max(entries.shape))
    beside = index_at[:main_axis] + [(index_at[main_axis] + 1) % entries.shape[main_axis]] + index_at[main_axis + 1:]
    return entries.at[tuple(index_at)].set(smallest).at[tuple(beside)].set(high)


def levels(rng, shape, shards, low, largest):
    factor_of = 1.0
    for axis_at, shards_of in shards:
        heights = jax.random.uniform(jax.random.fold_in(jax.random.fold_in(rng, 6), axis_at), (shards_of,), jnp.float32, low / len(shards), largest / len(shards))
        factor_of = factor_of * jnp.repeat(jnp.exp(heights), shape[axis_at] // shards_of).reshape((-1,) + (1,) * (len(shape) - 1 - axis_at))
    return factor_of


def scatter_about(rng, shape, width, most, shards=(), kind=jnp.bfloat16):
    entries = jax.random.normal(rng, shape, jnp.float32) * width
    if len(shards) > 0:
        entries = levels(rng, shape, shards, -0.22, 0.18) * entries
    return jnp.clip(entries, min=-most, max=most).astype(kind)


def setup_inputs(seed: int = 0) -> dict:
    arg_keys = jax.random.split(jax.random.key(seed), 10)
    return {
        "cotangent": scatter_about(arg_keys[0], (N_LAT, N_LON * BLK_DEV, CH, PTS), 1.0, 6.0, ((0, 4), (1, 8))),
        "tiles": scatter_about(arg_keys[1], (NTILES, PTS, PTS), (4 * PTS) ** -0.5, 0.25),
        "local_src": with_ends(jax.random.randint(arg_keys[2], (STEPS, N_LAT, N_LON * LOC), 0, BLK_DEV), jax.random.fold_in(arg_keys[2], 1), 0, BLK_DEV - 1).astype(jnp.int32),
        "local_tgt": with_ends(jax.random.randint(arg_keys[3], (STEPS, N_LAT, N_LON * LOC), 0, BLK_DEV), jax.random.fold_in(arg_keys[3], 1), 0, BLK_DEV - 1).astype(jnp.int32),
        "local_tile": with_ends(jax.random.randint(arg_keys[4], (STEPS, N_LAT, N_LON * LOC), 0, NTILES), jax.random.fold_in(arg_keys[4], 1), 0, NTILES - 1).astype(jnp.int32),
        "remote_src": with_ends(jax.random.randint(arg_keys[5], (STEPS, N_LAT, N_LON * SLOTS), 0, BLK_DEV), jax.random.fold_in(arg_keys[5], 1), 0, BLK_DEV - 1).astype(jnp.int32),
        "remote_tgt": with_ends(jax.random.randint(arg_keys[6], (STEPS, N_LAT, N_LON * SLOTS), 0, BLK_DEV), jax.random.fold_in(arg_keys[6], 1), 0, BLK_DEV - 1).astype(jnp.int32),
        "remote_tile": with_ends(jax.random.randint(arg_keys[7], (STEPS, N_LAT, N_LON * SLOTS), 0, NTILES), jax.random.fold_in(arg_keys[7], 1), 0, NTILES - 1).astype(jnp.int32),
        "remote_live": draw_remote_live(jax.random.fold_in(arg_keys[9], 71), 0),
    }


def entry_lists(section, local_src, local_tgt, local_tile, remote_src, remote_tgt, remote_tile, remote_live):
    block_bases = ((jnp.arange(N_LAT, dtype=jnp.int32)[:, None] * N_LON + jnp.arange(N_LON, dtype=jnp.int32)[None, :]) * BLK_DEV).astype(jnp.int32)
    own_src = (local_src[section].reshape(N_LAT, N_LON, LOC) + block_bases[:, :, None]).reshape(-1)
    own_tgt = (local_tgt[section].reshape(N_LAT, N_LON, LOC) + block_bases[:, :, None]).reshape(-1)
    own_tile = local_tile[section].reshape(-1)
    own_weight = jnp.ones(own_src.shape, jnp.float32)
    slot_shape = (N_LAT, N_LON, N_LON, 3, CAP)
    band_index = lax.broadcasted_iota(jnp.int32, slot_shape, 0)
    owner_sector = lax.broadcasted_iota(jnp.int32, slot_shape, 2)
    offset = lax.broadcasted_iota(jnp.int32, slot_shape, 3)
    owner_band = band_index + offset - 1
    owner_band = jnp.where((owner_band < 0) | (owner_band >= N_LAT), band_index, owner_band)
    far_src = ((owner_band * N_LON + owner_sector) * BLK_DEV + remote_src[section].reshape(slot_shape)).reshape(-1)
    far_tgt = (remote_tgt[section].reshape(slot_shape) + block_bases[:, :, None, None, None]).reshape(-1)
    far_tile = remote_tile[section].reshape(-1)
    far_weight = remote_live[section].reshape(-1).astype(jnp.float32)
    sources = jnp.concatenate([own_src, far_src]).astype(jnp.int32)
    targets = jnp.concatenate([own_tgt, far_tgt]).astype(jnp.int32)
    tile_ids = jnp.concatenate([own_tile, far_tile]).astype(jnp.int32)
    weights = jnp.concatenate([own_weight, far_weight])
    return sources, targets, tile_ids, weights


def apply_adjoint(field_flat, lists, tiles):
    sources, targets, tile_ids, weights = lists
    entry_count = sources.shape[0]
    block_size = math.gcd(entry_count, 2048)

    def advance(summed, pieces):
        src_ids, tgt_ids, tile_pick, weighting = pieces
        gathered = field_flat[tgt_ids].astype(jnp.float32)
        matrices = tiles[tile_pick].astype(jnp.float32)
        contrib = jnp.einsum("ecj,eij->eci", gathered, matrices, precision=lax.Precision.HIGHEST)
        contrib = contrib * weighting[:, None, None]
        return summed.at[src_ids].add(contrib), None

    start = jnp.zeros(field_flat.shape, jnp.float32)
    pieces = (sources.reshape(-1, block_size), targets.reshape(-1, block_size),
              tile_ids.reshape(-1, block_size), weights.reshape(-1, block_size))
    summed, _ = lax.scan(advance, start, pieces)
    return summed


def reference(cotangent, tiles, local_src, local_tgt, local_tile, remote_src, remote_tgt, remote_tile, remote_live):
    field_flat = cotangent.reshape(N_LAT * N_LON * BLK_DEV, CH, PTS)
    later = entry_lists(1, local_src, local_tgt, local_tile, remote_src, remote_tgt, remote_tile, remote_live)
    middle_sum = apply_adjoint(field_flat, later, tiles)
    middle = middle_sum.astype(jnp.bfloat16)
    earlier = entry_lists(0, local_src, local_tgt, local_tile, remote_src, remote_tgt, remote_tile, remote_live)
    result = apply_adjoint(middle, earlier, tiles)
    return result.reshape(N_LAT, N_LON * BLK_DEV, CH, PTS)
```

```python
import functools
import math

import jax
import jax.numpy as jnp
from jax import lax
from jax.experimental import pallas as pl
from jax.experimental.pallas import tpu as pltpu
from jax.sharding import PartitionSpec as P

MESH = pl.DeviceIdType.MESH
SHIFT = 7
MASK = (1 << SHIFT) - 1
LIMIT = 56 * 1024 * 1024


def product(block, tile):
    return lax.dot_general(
        block, tile, (((1,), (1,)), ((), ())), preferred_element_type=jnp.float32
    )


def exchange_kernel(
    bands,
    sectors,
    first,
    own_ref,
    far_tgt_ref,
    field_ref,
    tiles_ref,
    codes_ref,
    own_out,
    far_out,
    *rest,
):
    if first:
        codes_out, stage, recv, codes_in, codes, send_sem, recv_sem, code_send, code_recv, code_sem = rest
    else:
        stage, recv, send_sem, recv_sem = rest
        codes = codes_ref
    cells, cap = stage.shape[0], stage.shape[1]
    lane0 = 0 if first else cap
    band = lax.axis_index("lat")
    sector = lax.axis_index("lon")

    def offset_of(turn):
        turn_at = lax.div(turn + 1, 2)
        return sectors // 2 + turn_at * (1 - 2 * lax.rem(turn, 2))

    def out_cell(step):
        d = lax.rem(step, 3)
        to_sector = lax.rem(sector + offset_of(lax.div(step, 3)) + sectors, sectors)
        band_at = band + d - 1
        outside = jnp.logical_or(band_at < 0, band_at >= bands)
        to_band = jnp.where(outside, band, band_at)
        slot = jnp.where(outside, 2 - d, d)
        mine = jnp.logical_and(to_sector == sector, to_band == band)
        return to_sector * 3 + d, sector * 3 + slot, to_band, to_sector, mine

    def in_cell(step):
        slot = lax.rem(step, 3)
        of_sector = lax.rem(sector - offset_of(lax.div(step, 3)) + 2 * sectors, sectors)
        band_at = band + 1 - slot
        outside = jnp.logical_or(band_at < 0, band_at >= bands)
        of_band = jnp.where(outside, band, band_at)
        mine = jnp.logical_and(of_sector == sector, of_band == band)
        return of_sector * 3 + slot, mine

    barrier = pltpu.get_barrier_semaphore()

    def greet(step, carry):
        to_sector = lax.div(step, 3)
        to_band = band + lax.rem(step, 3) - 1
        inside = jnp.logical_and(to_band >= 0, to_band < bands)
        other = jnp.logical_not(jnp.logical_and(to_sector == sector, to_band == band))

        @pl.when(jnp.logical_and(inside, other))
        def _():
            pl.semaphore_signal(barrier, inc=1, device_id=(to_band, to_sector), device_id_type=MESH)

        return carry

    lax.fori_loop(0, cells, greet, 0)
    below = jnp.where(band > 0, 1, 0)
    above = jnp.where(band < bands - 1, 1, 0)
    pl.semaphore_wait(barrier, (1 + below + above) * sectors - 1)

    def data_copy(src, dst, to_band, to_sector):
        return pltpu.make_async_remote_copy(
            src_ref=stage.at[src],
            dst_ref=recv.at[dst],
            send_sem=send_sem.at[src],
            recv_sem=recv_sem.at[dst],
            device_id=(to_band, to_sector),
            device_id_type=MESH,
        )

    def code_copy(src, dst, to_band, to_sector):
        return pltpu.make_async_remote_copy(
            src_ref=codes_ref.at[src],
            dst_ref=codes_in.at[dst],
            send_sem=code_send.at[src],
            recv_sem=code_recv.at[dst],
            device_id=(to_band, to_sector),
            device_id_type=MESH,
        )

    def send(step, carry):
        src, dst, to_band, to_sector, mine = out_cell(step)
        if first:

            @pl.when(mine)
            def _():
                codes_in[dst] = codes_ref[src]

            @pl.when(jnp.logical_not(mine))
            def _():
                code_copy(src, dst, to_band, to_sector).start()

        for k in range(cap):
            stage[src, k] = field_ref[far_tgt_ref[src * cap + k]]

        @pl.when(mine)
        def _():
            recv[dst] = stage[src]

        @pl.when(jnp.logical_not(mine))
        def _():
            data_copy(src, dst, to_band, to_sector).start()

        return carry

    lax.fori_loop(0, cells, send, 0)

    own = own_ref.shape[0]
    group = math.gcd(own, 16)

    def own_products(step, carry):
        for k in range(group):
            at = step * group + k
            code = own_ref[at]
            own_out[at] = product(field_ref[code & MASK], tiles_ref[code >> SHIFT])
        return carry

    lax.fori_loop(0, own // group, own_products, 0)

    if first:

        def code_wait(step, carry):
            dst, mine = in_cell(step)

            @pl.when(jnp.logical_not(mine))
            def _():
                code_copy(dst, dst, band, sector).wait_recv()

            return carry

        lax.fori_loop(0, cells, code_wait, 0)
        local = pltpu.make_async_copy(codes_in, codes, code_sem)
        local.start()
        codes_out[...] = codes_in[...]
        local.wait()

    def far_products(step, carry):
        dst, mine = in_cell(step)

        @pl.when(jnp.logical_not(mine))
        def _():
            data_copy(dst, dst, band, sector).wait_recv()

        for k in range(cap):
            code = codes[dst, 0, lane0 + k]
            far_out[dst, k] = product(recv[dst, k], tiles_ref[code >> SHIFT])
        return carry

    lax.fori_loop(0, cells, far_products, 0)

    def drain(step, carry):
        src, dst, to_band, to_sector, mine = out_cell(step)

        @pl.when(jnp.logical_not(mine))
        def _():
            data_copy(src, dst, to_band, to_sector).wait_send()
            if first:
                code_copy(src, dst, to_band, to_sector).wait_send()

        return carry

    lax.fori_loop(0, cells, drain, 0)


def exchange(bands, sectors, first, own_codes, far_tgt, field, tiles, codes):
    cells = sectors * 3
    cap = far_tgt.shape[0] // cells
    block = field.shape[1:]
    smem = pl.BlockSpec(memory_space=pltpu.SMEM)
    vmem = pl.BlockSpec(memory_space=pltpu.VMEM)
    outs = [
        jax.ShapeDtypeStruct((own_codes.shape[0],) + block, jnp.float32),
        jax.ShapeDtypeStruct((cells, cap) + block, jnp.float32),
    ]
    scratch = [
        pltpu.VMEM((cells, cap) + block, jnp.bfloat16),
        pltpu.VMEM((cells, cap) + block, jnp.bfloat16),
    ]
    sems = [pltpu.SemaphoreType.DMA((cells,)), pltpu.SemaphoreType.DMA((cells,))]
    if first:
        outs.append(jax.ShapeDtypeStruct(codes.shape, jnp.int32))
        scratch += [pltpu.VMEM(codes.shape, jnp.int32), pltpu.SMEM(codes.shape, jnp.int32)]
        sems += [
            pltpu.SemaphoreType.DMA((cells,)),
            pltpu.SemaphoreType.DMA((cells,)),
            pltpu.SemaphoreType.DMA,
        ]
    entries = own_codes.shape[0] + far_tgt.shape[0]
    return pl.pallas_call(
        functools.partial(exchange_kernel, bands, sectors, first),
        out_shape=outs,
        in_specs=[smem, smem, vmem, vmem, vmem if first else smem],
        out_specs=[vmem] * len(outs),
        scratch_shapes=scratch + sems,
        compiler_params=pltpu.CompilerParams(
            collective_id=0 if first else 1, has_side_effects=True, vmem_limit_bytes=LIMIT
        ),
        cost_estimate=pl.CostEstimate(
            flops=2 * entries * block[0] * block[1] * block[1],
            bytes_accessed=entries * block[0] * block[1] * 8,
            transcendentals=0,
        ),
        name="exchange",
    )(own_codes, far_tgt, field, tiles, codes)


def gather_kernel(lane0, own_ref, codes_ref, own_values, far_values, out_ref, total):
    total[...] = jnp.zeros_like(total)
    own = own_ref.shape[0]
    group = math.gcd(own, 16)
    cells, cap = far_values.shape[0], far_values.shape[1]

    def own_add(step, carry):
        for k in range(group):
            at = step * group + k
            total[own_ref[at]] += own_values[at]
        return carry

    lax.fori_loop(0, own // group, own_add, 0)

    def far_add(cell, carry):
        for k in range(cap):
            total[codes_ref[cell, 0, lane0 + k] & MASK] += far_values[cell, k]
        return carry

    lax.fori_loop(0, cells, far_add, 0)
    out_ref[...] = total[0 : out_ref.shape[0]].astype(out_ref.dtype)


def gather(lane0, own_src, codes, own_values, far_values, blocks, kind):
    block = own_values.shape[1:]
    smem = pl.BlockSpec(memory_space=pltpu.SMEM)
    vmem = pl.BlockSpec(memory_space=pltpu.VMEM)
    return pl.pallas_call(
        functools.partial(gather_kernel, lane0),
        out_shape=jax.ShapeDtypeStruct((blocks,) + block, kind),
        in_specs=[smem, smem, vmem, vmem],
        out_specs=vmem,
        scratch_shapes=[pltpu.VMEM((blocks + 1,) + block, jnp.float32)],
        compiler_params=pltpu.CompilerParams(vmem_limit_bytes=LIMIT),
        name="gather",
    )(own_src, codes, own_values, far_values)


def on_device(
    bands,
    sectors,
    cotangent,
    tiles,
    local_src,
    local_tgt,
    local_tile,
    remote_src,
    remote_tgt,
    remote_tile,
    remote_live,
):
    field = cotangent[0]
    blocks = field.shape[0]
    cells = sectors * 3
    cap = remote_src.shape[2] // cells
    own_codes = local_tgt[:, 0] + (local_tile[:, 0] << SHIFT)
    source = jnp.where(remote_live[:, 0] > 0, remote_src[:, 0], blocks)
    far_codes = (source + (remote_tile[:, 0] << SHIFT)).reshape(2, cells, cap)
    codes = jnp.concatenate([far_codes[1], far_codes[0]], 1)
    codes = jnp.pad(codes, ((0, 0), (0, 128 - 2 * cap)))[:, None, :]
    for section in (1, 0):
        first = section == 1
        got = exchange(
            bands, sectors, first, own_codes[section], remote_tgt[section, 0], field, tiles, codes
        )
        if first:
            codes = got[2]
        field = gather(
            0 if first else cap,
            local_src[section, 0],
            codes,
            got[0],
            got[1],
            blocks,
            jnp.bfloat16 if first else jnp.float32,
        )
    return field[None]


def solution(mesh):
    placed = (P("lat", "lon", None, None), P()) + (P(None, "lat", "lon"),) * 7
    return jax.shard_map(
        functools.partial(on_device, mesh.shape["lat"], mesh.shape["lon"]),
        mesh=mesh,
        in_specs=placed,
        out_specs=P("lat", "lon", None, None),
        check_vma=False,
    )
```

```python
import functools
import math

import jax
import jax.numpy as jnp
from jax import lax
from jax.experimental import pallas as pl
from jax.experimental.pallas import tpu as pltpu
from jax.sharding import PartitionSpec as P

MESH = pl.DeviceIdType.MESH
SHIFT = 7
MASK = (1 << SHIFT) - 1
LIMIT = 56 * 1024 * 1024


def product(block, tile):
    return lax.dot_general(
        block, tile, (((1,), (1,)), ((), ())), preferred_element_type=jnp.float32
    )


def split(value):
    high = value.astype(jnp.bfloat16)
    return high, (value - high.astype(jnp.float32)).astype(jnp.bfloat16)


def steps_kernel(
    bands,
    sectors,
    own_ref,
    far_tgt_ref,
    own_src_ref,
    codes_ref,
    cotangent_ref,
    tiles_ref,
    out_ref,
    middle,
    stage,
    recv,
    codes_in,
    codes,
    own_values,
    far_values,
    picks,
    total,
    send_sem,
    recv_sem,
    code_send,
    code_recv,
    code_sem,
):
    cells, cap = stage.shape[0], stage.shape[1]
    blocks, channels, points = cotangent_ref.shape
    own = own_ref.shape[1]
    own_group = math.gcd(own, 16)
    rows = far_values.shape[0] // channels
    pad = rows // cells
    chunk = math.gcd(rows, 128)
    band = lax.axis_index("lat")
    sector = lax.axis_index("lon")

    def offset_of(turn):
        turn_at = lax.div(turn + 1, 2)
        return sectors // 2 + turn_at * (1 - 2 * lax.rem(turn, 2))

    def out_cell(step):
        d = lax.rem(step, 3)
        to_sector = lax.rem(sector + offset_of(lax.div(step, 3)) + sectors, sectors)
        band_at = band + d - 1
        outside = jnp.logical_or(band_at < 0, band_at >= bands)
        to_band = jnp.where(outside, band, band_at)
        slot = jnp.where(outside, 2 - d, d)
        mine = jnp.logical_and(to_sector == sector, to_band == band)
        return to_sector * 3 + d, sector * 3 + slot, to_band, to_sector, mine

    def in_cell(step):
        slot = lax.rem(step, 3)
        of_sector = lax.rem(sector - offset_of(lax.div(step, 3)) + 2 * sectors, sectors)
        band_at = band + 1 - slot
        outside = jnp.logical_or(band_at < 0, band_at >= bands)
        of_band = jnp.where(outside, band, band_at)
        mine = jnp.logical_and(of_sector == sector, of_band == band)
        return of_sector * 3 + slot, mine

    barrier = pltpu.get_barrier_semaphore()

    def greet(step, carry):
        to_sector = lax.div(step, 3)
        to_band = band + lax.rem(step, 3) - 1
        inside = jnp.logical_and(to_band >= 0, to_band < bands)
        other = jnp.logical_not(jnp.logical_and(to_sector == sector, to_band == band))

        @pl.when(jnp.logical_and(inside, other))
        def _():
            pl.semaphore_signal(barrier, inc=1, device_id=(to_band, to_sector), device_id_type=MESH)

        return carry

    lax.fori_loop(0, cells, greet, 0)
    below = jnp.where(band > 0, 1, 0)
    above = jnp.where(band < bands - 1, 1, 0)
    pl.semaphore_wait(barrier, (1 + below + above) * sectors - 1)

    def code_copy(src, dst, to_band, to_sector):
        return pltpu.make_async_remote_copy(
            src_ref=codes_ref.at[src],
            dst_ref=codes_in.at[dst],
            send_sem=code_send.at[src],
            recv_sem=code_recv.at[dst],
            device_id=(to_band, to_sector),
            device_id_type=MESH,
        )

    for turn, section in enumerate((1, 0)):
        first = turn == 0
        field_ref = cotangent_ref if first else middle

        def data_copy(src, dst, to_band, to_sector):
            return pltpu.make_async_remote_copy(
                src_ref=stage.at[src],
                dst_ref=recv.at[turn, dst],
                send_sem=send_sem.at[turn, src],
                recv_sem=recv_sem.at[turn, dst],
                device_id=(to_band, to_sector),
                device_id_type=MESH,
            )

        def send(step, carry):
            src, dst, to_band, to_sector, mine = out_cell(step)
            for k in range(cap):
                stage[src, k] = field_ref[far_tgt_ref[section, src * cap + k]]

            @pl.when(mine)
            def _():
                recv[turn, dst] = stage[src]
                if first:
                    codes_in[dst] = codes_ref[src]

            @pl.when(jnp.logical_not(mine))
            def _():
                if first:
                    code_copy(src, dst, to_band, to_sector).start()
                data_copy(src, dst, to_band, to_sector).start()

            return carry

        lax.fori_loop(0, cells, send, 0)

        if first:
            far_values[...] = jnp.zeros_like(far_values)

        def own_products(step, carry):
            for k in range(own_group):
                at = step * own_group + k
                code = own_ref[section, at]
                own_values[pl.ds(at, channels, stride=own), :] = product(
                    field_ref[code & MASK], tiles_ref[code >> SHIFT]
                )
            return carry

        lax.fori_loop(0, own // own_group, own_products, 0)

        block_ids = lax.broadcasted_iota(jnp.int32, (blocks, own), 0)
        own_pick = (block_ids == own_src_ref[section]).astype(jnp.float32).astype(jnp.bfloat16)

        def own_sum(c, carry):
            high, low = split(own_values[pl.ds(pl.multiple_of(c * own, 8), own), :])
            both = jnp.dot(
                own_pick,
                jnp.concatenate([high, low], 1),
                preferred_element_type=jnp.float32,
            )
            total[pl.ds(pl.multiple_of(c * blocks, 8), blocks), :] = (
                both[:, :points] + both[:, points:]
            )
            return carry

        lax.fori_loop(0, channels, own_sum, 0)

        if first:

            def code_wait(step, carry):
                dst, mine = in_cell(step)

                @pl.when(jnp.logical_not(mine))
                def _():
                    code_copy(dst, dst, band, sector).wait_recv()

                return carry

            lax.fori_loop(0, cells, code_wait, 0)
            local = pltpu.make_async_copy(codes_in, codes, code_sem)
            local.start()
            local.wait()

        row_ids = lax.broadcasted_iota(jnp.int32, (pad, points), 0)
        lane_ids = lax.broadcasted_iota(jnp.int32, (pad, points), 1)

        def far_products(step, carry):
            dst, mine = in_cell(step)

            @pl.when(jnp.logical_not(mine))
            def _():
                data_copy(dst, dst, band, sector).wait_recv()

            wanted = jnp.full((pad, points), -1, jnp.int32)
            for k in range(cap):
                code = codes[dst, 0, turn * cap + k]
                far_values[pl.ds(step * pad + k, channels, stride=rows), :] = product(
                    recv[turn, dst, k], tiles_ref[code >> SHIFT]
                )
                wanted = jnp.where(row_ids == k, code & MASK, wanted)
            picks[pl.ds(pl.multiple_of(step * pad, pad), pad), :] = (wanted == lane_ids).astype(
                jnp.float32
            )
            return carry

        per_chunk = chunk // pad
        for part in range(rows // chunk):
            lax.fori_loop(part * per_chunk, (part + 1) * per_chunk, far_products, 0)
            pick = picks[part * chunk : (part + 1) * chunk, :].T[:blocks].astype(jnp.bfloat16)
            pick = jnp.concatenate([pick, pick], 1)

            def far_sum(pair, carry):
                parts = []
                for c in range(2):
                    at = pl.multiple_of((pair * 2 + c) * rows + part * chunk, 8)
                    parts.append(jnp.concatenate(split(far_values[pl.ds(at, chunk), :]), 0))
                both = jnp.dot(
                    pick, jnp.concatenate(parts, 1), preferred_element_type=jnp.float32
                )
                for c in range(2):
                    at = pl.multiple_of((pair * 2 + c) * blocks, 8)
                    total[pl.ds(at, blocks), :] += both[:, c * points : (c + 1) * points]
                return carry

            lax.fori_loop(0, channels // 2, far_sum, 0, unroll=4)

        def drain(step, carry):
            src, dst, to_band, to_sector, mine = out_cell(step)

            @pl.when(jnp.logical_not(mine))
            def _():
                data_copy(src, dst, to_band, to_sector).wait_send()
                if first:
                    code_copy(src, dst, to_band, to_sector).wait_send()

            return carry

        lax.fori_loop(0, cells, drain, 0)

        def finish(step, carry):
            for k in range(8):
                n = step * 8 + k
                value = total[pl.ds(n, channels, stride=blocks), :]
                if first:
                    middle[n] = value.astype(jnp.bfloat16)
                else:
                    out_ref[n] = value
            return carry

        lax.fori_loop(0, blocks // 8, finish, 0)


def both_steps(bands, sectors, own_codes, far_tgt, own_src, codes, field, tiles):
    cells = sectors * 3
    cap = far_tgt.shape[1] // cells
    pad = (cap + 15) // 16 * 16
    blocks, channels, points = field.shape
    own = own_codes.shape[1]
    smem = pl.BlockSpec(memory_space=pltpu.SMEM)
    vmem = pl.BlockSpec(memory_space=pltpu.VMEM)
    dma = pltpu.SemaphoreType.DMA
    entries = 2 * (own + far_tgt.shape[1])
    return pl.pallas_call(
        functools.partial(steps_kernel, bands, sectors),
        out_shape=jax.ShapeDtypeStruct(field.shape, jnp.float32),
        in_specs=[smem, smem, vmem, vmem, vmem, vmem],
        out_specs=vmem,
        scratch_shapes=[
            pltpu.VMEM(field.shape, jnp.bfloat16),
            pltpu.VMEM((cells, cap, channels, points), jnp.bfloat16),
            pltpu.VMEM((2, cells, cap, channels, points), jnp.bfloat16),
            pltpu.VMEM(codes.shape, jnp.int32),
            pltpu.SMEM(codes.shape, jnp.int32),
            pltpu.VMEM((channels * own, points), jnp.float32),
            pltpu.VMEM((channels * cells * pad, points), jnp.float32),
            pltpu.VMEM((cells * pad, points), jnp.float32),
            pltpu.VMEM((channels * blocks, points), jnp.float32),
            dma((2, cells)),
            dma((2, cells)),
            dma((cells,)),
            dma((cells,)),
            dma,
        ],
        compiler_params=pltpu.CompilerParams(
            collective_id=0, has_side_effects=True, vmem_limit_bytes=LIMIT
        ),
        cost_estimate=pl.CostEstimate(
            flops=2 * entries * channels * points * points,
            bytes_accessed=entries * channels * points * 8,
            transcendentals=0,
        ),
        name="both_steps",
    )(own_codes, far_tgt, own_src, codes, field, tiles)


def on_device(
    bands,
    sectors,
    cotangent,
    tiles,
    local_src,
    local_tgt,
    local_tile,
    remote_src,
    remote_tgt,
    remote_tile,
    remote_live,
):
    field = cotangent[0]
    blocks = field.shape[0]
    cells = sectors * 3
    cap = remote_src.shape[2] // cells
    own_codes = local_tgt[:, 0] + (local_tile[:, 0] << SHIFT)
    source = jnp.where(remote_live[:, 0] > 0, remote_src[:, 0], blocks)
    far_codes = (source + (remote_tile[:, 0] << SHIFT)).reshape(2, cells, cap)
    codes = jnp.concatenate([far_codes[1], far_codes[0]], 1)
    codes = jnp.pad(codes, ((0, 0), (0, 128 - 2 * cap)))[:, None, :]
    summed = both_steps(
        bands, sectors, own_codes, remote_tgt[:, 0], local_src, codes, field, tiles
    )
    return summed[None]


def solution(mesh):
    placed = (P("lat", "lon", None, None), P()) + (P(None, "lat", "lon"),) * 7
    return jax.shard_map(
        functools.partial(on_device, mesh.shape["lat"], mesh.shape["lon"]),
        mesh=mesh,
        in_specs=placed,
        out_specs=P("lat", "lon", None, None),
        check_vma=False,
    )
```

```python
import functools
import math

import jax
import jax.numpy as jnp
from jax import lax
from jax.experimental import pallas as pl
from jax.experimental.pallas import tpu as pltpu
from jax.sharding import PartitionSpec as P

MESH = pl.DeviceIdType.MESH
SHIFT = 7
MASK = (1 << SHIFT) - 1
LIMIT = 56 * 1024 * 1024


def product(block, tile):
    return lax.dot_general(
        block, tile, (((1,), (1,)), ((), ())), preferred_element_type=jnp.float32
    )


def split(value):
    high = value.astype(jnp.bfloat16)
    return high, (value - high.astype(jnp.float32)).astype(jnp.bfloat16)


def steps_kernel(
    bands,
    sectors,
    own_ref,
    far_tgt_ref,
    own_src_ref,
    codes_ref,
    targets_ref,
    cotangent_ref,
    tiles_ref,
    out_ref,
    middle,
    stage,
    recv,
    codes_in,
    codes,
    passing_first,
    passing_second,
    targets_in,
    targets,
    own_values,
    far_values,
    picks,
    total,
    send_sem,
    recv_sem,
    code_send,
    code_recv,
    code_sem,
    field_send,
    field_recv,
    target_send,
    target_recv,
):
    cells, cap = stage.shape[0], stage.shape[1]
    blocks, channels, points = cotangent_ref.shape
    own = own_ref.shape[1]
    own_group = math.gcd(own, 16)
    rows = far_values.shape[0] // channels
    pad = rows // cells
    chunk = math.gcd(rows, 128)
    band = lax.axis_index("lat")
    sector = lax.axis_index("lon")

    half = sectors // 2
    near_steps = 3 * half
    base = lax.div(sector, half) * half
    other_base = half - base
    partner = lax.rem(sector + half, sectors)
    relays = lax.rem(band, 2) == 0

    def landing(d, to_sector):
        band_at = band + d - 1
        outside = jnp.logical_or(band_at < 0, band_at >= bands)
        to_band = jnp.where(outside, band, band_at)
        slot = jnp.where(outside, 2 - d, d)
        mine = jnp.logical_and(to_sector == sector, to_band == band)
        return slot, to_band, mine

    def origin(slot):
        band_at = band + 1 - slot
        outside = jnp.logical_or(band_at < 0, band_at >= bands)
        return jnp.where(outside, band, band_at)

    def out_cell(step):
        d = lax.rem(step, 3)
        near = base + lax.rem(sector + lax.div(step, 3), half)
        far = other_base + lax.rem(sector + lax.div(step, 3), half)
        crosses = step >= near_steps
        passes_on = jnp.logical_and(crosses, relays)
        to_sector = jnp.where(jnp.logical_and(crosses, jnp.logical_not(relays)), far, near)
        held = jnp.where(crosses, far, near)
        of_sector = jnp.where(passes_on, partner, sector)
        slot, to_band, mine = landing(d, to_sector)
        return held * 3 + d, to_sector * 3 + d, of_sector * 3 + slot, to_band, to_sector, mine

    def in_cell(step):
        slot = lax.rem(step, 3)
        turned = lax.rem(sector - lax.div(step, 3) + 2 * sectors, half)
        crosses = step >= near_steps
        of_sector = jnp.where(crosses, other_base, base) + turned
        of_band = origin(slot)
        passed_on = jnp.logical_and(crosses, lax.rem(of_band, 2) == 0)
        via = jnp.where(passed_on, lax.rem(of_sector + half, sectors), of_sector)
        mine = jnp.logical_and(via == sector, of_band == band)
        return of_sector * 3 + slot, mine

    barrier = pltpu.get_barrier_semaphore()

    def greet(step, carry):
        to_sector = lax.div(step, 3)
        to_band = band + lax.rem(step, 3) - 1
        inside = jnp.logical_and(to_band >= 0, to_band < bands)
        other = jnp.logical_not(jnp.logical_and(to_sector == sector, to_band == band))

        @pl.when(jnp.logical_and(inside, other))
        def _():
            pl.semaphore_signal(barrier, inc=1, device_id=(to_band, to_sector), device_id_type=MESH)

        return carry

    lax.fori_loop(0, cells, greet, 0)
    below = jnp.where(band > 0, 1, 0)
    above = jnp.where(band < bands - 1, 1, 0)
    pl.semaphore_wait(barrier, (1 + below + above) * sectors - 1)

    def code_copy(src, dst, to_band, to_sector):
        return pltpu.make_async_remote_copy(
            src_ref=codes_ref.at[src],
            dst_ref=codes_in.at[dst],
            send_sem=code_send.at[src],
            recv_sem=code_recv.at[dst],
            device_id=(to_band, to_sector),
            device_id_type=MESH,
        )

    def target_copy():
        return pltpu.make_async_remote_copy(
            src_ref=targets_ref,
            dst_ref=targets_in,
            send_sem=target_send,
            recv_sem=target_recv,
            device_id=(band, partner),
            device_id_type=MESH,
        )

    def code_out(cell):
        to_sector = lax.div(cell, 3)
        slot, to_band, mine = landing(lax.rem(cell, 3), to_sector)
        return code_copy(cell, sector * 3 + slot, to_band, to_sector), sector * 3 + slot, mine

    def send_codes(cell, carry):
        copy, dst, mine = code_out(cell)

        @pl.when(mine)
        def _():
            codes_in[dst] = codes_ref[cell]

        @pl.when(jnp.logical_not(mine))
        def _():
            copy.start()

        return carry

    def wait_codes(cell, carry):
        mine = jnp.logical_and(lax.div(cell, 3) == sector, origin(lax.rem(cell, 3)) == band)

        @pl.when(jnp.logical_not(mine))
        def _():
            code_copy(cell, cell, band, sector).wait_recv()

        return carry

    def drain_codes(cell, carry):
        copy, _, mine = code_out(cell)

        @pl.when(jnp.logical_not(mine))
        def _():
            copy.wait_send()

        return carry

    for turn, section in enumerate((1, 0)):
        first = turn == 0
        field_ref = cotangent_ref if first else middle
        passing = passing_first if first else passing_second

        def data_copy(src, dst, to_band, to_sector):
            return pltpu.make_async_remote_copy(
                src_ref=stage.at[src],
                dst_ref=recv.at[turn, dst],
                send_sem=send_sem.at[turn, src],
                recv_sem=recv_sem.at[turn, dst],
                device_id=(to_band, to_sector),
                device_id_type=MESH,
            )

        def field_copy():
            return pltpu.make_async_remote_copy(
                src_ref=field_ref,
                dst_ref=passing,
                send_sem=field_send.at[turn],
                recv_sem=field_recv.at[turn],
                device_id=(band, partner),
                device_id_type=MESH,
            )

        def put(step, blocks_ref, pick_target):
            held, listed, dst, to_band, to_sector, mine = out_cell(step)
            for k in range(cap):
                stage[held, k] = blocks_ref[pick_target(listed * cap + k)]

            @pl.when(mine)
            def _():
                recv[turn, dst] = stage[held]

            @pl.when(jnp.logical_not(mine))
            def _():
                data_copy(held, dst, to_band, to_sector).start()

        def send(step, carry):
            put(step, field_ref, lambda at: far_tgt_ref[section, at])
            return carry

        def pass_on(step, carry):
            put(step, passing, lambda at: targets[section, 0, at])
            return carry

        @pl.when(relays)
        def _():
            field_copy().start()
            if first:
                target_copy().start()

        lax.fori_loop(0, near_steps, send, 0)

        if first:
            lax.fori_loop(0, cells, send_codes, 0)

        if first:
            far_values[...] = jnp.zeros_like(far_values)

        def own_products(step, carry):
            for k in range(own_group):
                at = step * own_group + k
                code = own_ref[section, at]
                own_values[pl.ds(at, channels, stride=own), :] = product(
                    field_ref[code & MASK], tiles_ref[code >> SHIFT]
                )
            return carry

        lax.fori_loop(0, own // own_group, own_products, 0)

        block_ids = lax.broadcasted_iota(jnp.int32, (blocks, own), 0)
        own_pick = (block_ids == own_src_ref[section]).astype(jnp.float32).astype(jnp.bfloat16)

        def own_sum(c, carry):
            high, low = split(own_values[pl.ds(pl.multiple_of(c * own, 8), own), :])
            both = jnp.dot(
                own_pick,
                jnp.concatenate([high, low], 1),
                preferred_element_type=jnp.float32,
            )
            total[pl.ds(pl.multiple_of(c * blocks, 8), blocks), :] = (
                both[:, :points] + both[:, points:]
            )
            return carry

        lax.fori_loop(0, channels, own_sum, 0)

        @pl.when(jnp.logical_not(relays))
        def _():
            lax.fori_loop(near_steps, cells, send, 0)


        if first:
            lax.fori_loop(0, cells, wait_codes, 0)
            local = pltpu.make_async_copy(codes_in, codes, code_sem)
            local.start()
            local.wait()

        row_ids = lax.broadcasted_iota(jnp.int32, (pad, points), 0)
        lane_ids = lax.broadcasted_iota(jnp.int32, (pad, points), 1)

        def far_products(step, carry):
            dst, mine = in_cell(step)

            @pl.when(jnp.logical_not(mine))
            def _():
                data_copy(dst, dst, band, sector).wait_recv()

            wanted = jnp.full((pad, points), -1, jnp.int32)
            for k in range(cap):
                code = codes[dst, 0, turn * cap + k]
                far_values[pl.ds(step * pad + k, channels, stride=rows), :] = product(
                    recv[turn, dst, k], tiles_ref[code >> SHIFT]
                )
                wanted = jnp.where(row_ids == k, code & MASK, wanted)
            picks[pl.ds(pl.multiple_of(step * pad, pad), pad), :] = (wanted == lane_ids).astype(
                jnp.float32
            )
            return carry

        per_chunk = chunk // pad
        relay_part = near_steps // per_chunk
        for part in range(rows // chunk):
            if part == relay_part:

                @pl.when(relays)
                def _():
                    if first:
                        target_copy().wait_recv()
                        listed = pltpu.make_async_copy(targets_in, targets, code_sem)
                        listed.start()
                        listed.wait()
                    field_copy().wait_recv()
                    lax.fori_loop(near_steps, cells, pass_on, 0)

            lax.fori_loop(part * per_chunk, (part + 1) * per_chunk, far_products, 0)
            pick = picks[part * chunk : (part + 1) * chunk, :].T[:blocks].astype(jnp.bfloat16)
            pick = jnp.concatenate([pick, pick], 1)

            def far_sum(pair, carry):
                parts = []
                for c in range(2):
                    at = pl.multiple_of((pair * 2 + c) * rows + part * chunk, 8)
                    parts.append(jnp.concatenate(split(far_values[pl.ds(at, chunk), :]), 0))
                both = jnp.dot(
                    pick, jnp.concatenate(parts, 1), preferred_element_type=jnp.float32
                )
                for c in range(2):
                    at = pl.multiple_of((pair * 2 + c) * blocks, 8)
                    total[pl.ds(at, blocks), :] += both[:, c * points : (c + 1) * points]
                return carry

            lax.fori_loop(0, channels // 2, far_sum, 0, unroll=4)

        def drain(step, carry):
            held, _, dst, to_band, to_sector, mine = out_cell(step)

            @pl.when(jnp.logical_not(mine))
            def _():
                data_copy(held, dst, to_band, to_sector).wait_send()

            return carry

        lax.fori_loop(0, cells, drain, 0)

        @pl.when(relays)
        def _():
            field_copy().wait_send()
            if first:
                target_copy().wait_send()

        if first:
            lax.fori_loop(0, cells, drain_codes, 0)

        def finish(step, carry):
            for k in range(8):
                n = step * 8 + k
                value = total[pl.ds(n, channels, stride=blocks), :]
                if first:
                    middle[n] = value.astype(jnp.bfloat16)
                else:
                    out_ref[n] = value
            return carry

        lax.fori_loop(0, blocks // 8, finish, 0)


def both_steps(bands, sectors, own_codes, targets, own_src, codes, field, tiles):
    far_tgt = targets[:, 0]
    cells = sectors * 3
    cap = far_tgt.shape[1] // cells
    pad = (cap + 15) // 16 * 16
    blocks, channels, points = field.shape
    own = own_codes.shape[1]
    smem = pl.BlockSpec(memory_space=pltpu.SMEM)
    vmem = pl.BlockSpec(memory_space=pltpu.VMEM)
    dma = pltpu.SemaphoreType.DMA
    entries = 2 * (own + far_tgt.shape[1])
    return pl.pallas_call(
        functools.partial(steps_kernel, bands, sectors),
        out_shape=jax.ShapeDtypeStruct(field.shape, jnp.float32),
        in_specs=[smem, smem, vmem, vmem, vmem, vmem, vmem],
        out_specs=vmem,
        scratch_shapes=[
            pltpu.VMEM(field.shape, jnp.bfloat16),
            pltpu.VMEM((cells, cap, channels, points), jnp.bfloat16),
            pltpu.VMEM((2, cells, cap, channels, points), jnp.bfloat16),
            pltpu.VMEM(codes.shape, jnp.int32),
            pltpu.SMEM(codes.shape, jnp.int32),
            pltpu.VMEM(field.shape, jnp.bfloat16),
            pltpu.VMEM(field.shape, jnp.bfloat16),
            pltpu.VMEM(targets.shape, jnp.int32),
            pltpu.SMEM(targets.shape, jnp.int32),
            pltpu.VMEM((channels * own, points), jnp.float32),
            pltpu.VMEM((channels * cells * pad, points), jnp.float32),
            pltpu.VMEM((cells * pad, points), jnp.float32),
            pltpu.VMEM((channels * blocks, points), jnp.float32),
            dma((2, cells)),
            dma((2, cells)),
            dma((cells,)),
            dma((cells,)),
            dma,
            dma((2,)),
            dma((2,)),
            dma,
            dma,
        ],
        compiler_params=pltpu.CompilerParams(
            collective_id=0, has_side_effects=True, vmem_limit_bytes=LIMIT
        ),
        cost_estimate=pl.CostEstimate(
            flops=2 * entries * channels * points * points,
            bytes_accessed=entries * channels * points * 8,
            transcendentals=0,
        ),
        name="both_steps",
    )(own_codes, far_tgt, own_src, codes, targets, field, tiles)


def on_device(
    bands,
    sectors,
    cotangent,
    tiles,
    local_src,
    local_tgt,
    local_tile,
    remote_src,
    remote_tgt,
    remote_tile,
    remote_live,
):
    field = cotangent[0]
    blocks = field.shape[0]
    cells = sectors * 3
    cap = remote_src.shape[2] // cells
    own_codes = local_tgt[:, 0] + (local_tile[:, 0] << SHIFT)
    source = jnp.where(remote_live[:, 0] > 0, remote_src[:, 0], blocks)
    far_codes = (source + (remote_tile[:, 0] << SHIFT)).reshape(2, cells, cap)
    codes = jnp.concatenate([far_codes[1], far_codes[0]], 1)
    codes = jnp.pad(codes, ((0, 0), (0, 128 - 2 * cap)))[:, None, :]
    summed = both_steps(
        bands, sectors, own_codes, remote_tgt, local_src, codes, field, tiles
    )
    return summed[None]


def solution(mesh):
    placed = (P("lat", "lon", None, None), P()) + (P(None, "lat", "lon"),) * 7
    return jax.shard_map(
        functools.partial(on_device, mesh.shape["lat"], mesh.shape["lon"]),
        mesh=mesh,
        in_specs=placed,
        out_specs=P("lat", "lon", None, None),
        check_vma=False,
    )
```

```python
import functools
import math

import jax
import jax.numpy as jnp
from jax import lax
from jax.experimental import pallas as pl
from jax.experimental.pallas import tpu as pltpu
from jax.sharding import PartitionSpec as P

MESH = pl.DeviceIdType.MESH
SHIFT = 7
MASK = (1 << SHIFT) - 1
LIMIT = 56 * 1024 * 1024


def product(block, tile):
    return lax.dot_general(
        block, tile, (((1,), (1,)), ((), ())), preferred_element_type=jnp.float32
    )


def split(value):
    high = value.astype(jnp.bfloat16)
    return high, (value - high.astype(jnp.float32)).astype(jnp.bfloat16)


def steps_kernel(
    bands,
    sectors,
    own_ref,
    far_tgt_ref,
    own_src_ref,
    codes_ref,
    targets_ref,
    cotangent_ref,
    tiles_ref,
    out_ref,
    middle,
    stage,
    recv,
    codes_in,
    codes,
    passing_first,
    passing_second,
    targets_in,
    targets,
    own_values,
    far_values,
    picks,
    total,
    send_sem,
    recv_sem,
    code_send,
    code_recv,
    code_sem,
    field_send,
    field_recv,
    target_send,
    target_recv,
):
    cells, cap = stage.shape[0], stage.shape[1]
    blocks, channels, points = cotangent_ref.shape
    own = own_ref.shape[1]
    own_group = math.gcd(own, 16)
    rows = far_values.shape[0] // channels
    pad = rows // cells
    chunk = math.gcd(rows, 128)
    band = lax.axis_index("lat")
    sector = lax.axis_index("lon")

    half = sectors // 2
    near_steps = 3 * half
    base = lax.div(sector, half) * half
    other_base = half - base
    partner = lax.rem(sector + half, sectors)
    relays = lax.rem(band, 2) == 0

    def landing(d, to_sector):
        band_at = band + d - 1
        outside = jnp.logical_or(band_at < 0, band_at >= bands)
        to_band = jnp.where(outside, band, band_at)
        slot = jnp.where(outside, 2 - d, d)
        mine = jnp.logical_and(to_sector == sector, to_band == band)
        return slot, to_band, mine

    def origin(slot):
        band_at = band + 1 - slot
        outside = jnp.logical_or(band_at < 0, band_at >= bands)
        return jnp.where(outside, band, band_at)

    def out_cell(step):
        d = lax.rem(step, 3)
        near = base + lax.rem(sector + lax.div(step, 3), half)
        far = other_base + lax.rem(sector + lax.div(step, 3), half)
        crosses = step >= near_steps
        passes_on = jnp.logical_and(crosses, relays)
        to_sector = jnp.where(jnp.logical_and(crosses, jnp.logical_not(relays)), far, near)
        held = jnp.where(crosses, far, near)
        of_sector = jnp.where(passes_on, partner, sector)
        slot, to_band, mine = landing(d, to_sector)
        return held * 3 + d, to_sector * 3 + d, of_sector * 3 + slot, to_band, to_sector, mine

    def in_cell(step):
        slot = lax.rem(step, 3)
        turned = lax.rem(sector - lax.div(step, 3) + 2 * sectors, half)
        crosses = step >= near_steps
        of_sector = jnp.where(crosses, other_base, base) + turned
        of_band = origin(slot)
        passed_on = jnp.logical_and(crosses, lax.rem(of_band, 2) == 0)
        via = jnp.where(passed_on, lax.rem(of_sector + half, sectors), of_sector)
        mine = jnp.logical_and(via == sector, of_band == band)
        return of_sector * 3 + slot, mine

    barrier = pltpu.get_barrier_semaphore()

    def greet(step, carry):
        to_sector = lax.div(step, 3)
        to_band = band + lax.rem(step, 3) - 1
        inside = jnp.logical_and(to_band >= 0, to_band < bands)
        other = jnp.logical_not(jnp.logical_and(to_sector == sector, to_band == band))

        @pl.when(jnp.logical_and(inside, other))
        def _():
            pl.semaphore_signal(barrier, inc=1, device_id=(to_band, to_sector), device_id_type=MESH)

        return carry

    lax.fori_loop(0, cells, greet, 0)
    below = jnp.where(band > 0, 1, 0)
    above = jnp.where(band < bands - 1, 1, 0)
    pl.semaphore_wait(barrier, (1 + below + above) * sectors - 1)

    def code_copy(src, dst, to_band, to_sector):
        return pltpu.make_async_remote_copy(
            src_ref=codes_ref.at[src],
            dst_ref=codes_in.at[dst],
            send_sem=code_send.at[src],
            recv_sem=code_recv.at[dst],
            device_id=(to_band, to_sector),
            device_id_type=MESH,
        )

    def target_copy():
        return pltpu.make_async_remote_copy(
            src_ref=targets_ref,
            dst_ref=targets_in,
            send_sem=target_send,
            recv_sem=target_recv,
            device_id=(band, partner),
            device_id_type=MESH,
        )

    def code_out(cell):
        to_sector = lax.div(cell, 3)
        slot, to_band, mine = landing(lax.rem(cell, 3), to_sector)
        return code_copy(cell, sector * 3 + slot, to_band, to_sector), sector * 3 + slot, mine

    def send_codes(cell, carry):
        copy, dst, mine = code_out(cell)

        @pl.when(mine)
        def _():
            codes_in[dst] = codes_ref[cell]

        @pl.when(jnp.logical_not(mine))
        def _():
            copy.start()

        return carry

    def wait_codes(cell, carry):
        mine = jnp.logical_and(lax.div(cell, 3) == sector, origin(lax.rem(cell, 3)) == band)

        @pl.when(jnp.logical_not(mine))
        def _():
            code_copy(cell, cell, band, sector).wait_recv()

        return carry

    def drain_codes(cell, carry):
        copy, _, mine = code_out(cell)

        @pl.when(jnp.logical_not(mine))
        def _():
            copy.wait_send()

        return carry

    for turn, section in enumerate((1, 0)):
        first = turn == 0
        field_ref = cotangent_ref if first else middle
        passing = passing_first if first else passing_second

        def data_copy(src, dst, to_band, to_sector):
            return pltpu.make_async_remote_copy(
                src_ref=stage.at[src],
                dst_ref=recv.at[turn, dst],
                send_sem=send_sem.at[turn, src],
                recv_sem=recv_sem.at[turn, dst],
                device_id=(to_band, to_sector),
                device_id_type=MESH,
            )

        def field_copy():
            return pltpu.make_async_remote_copy(
                src_ref=field_ref,
                dst_ref=passing,
                send_sem=field_send.at[turn],
                recv_sem=field_recv.at[turn],
                device_id=(band, partner),
                device_id_type=MESH,
            )

        def put(step, blocks_ref, pick_target):
            held, listed, dst, to_band, to_sector, mine = out_cell(step)
            for k in range(cap):
                stage[held, k] = blocks_ref[pick_target(listed * cap + k)]

            @pl.when(mine)
            def _():
                recv[turn, dst] = stage[held]

            @pl.when(jnp.logical_not(mine))
            def _():
                data_copy(held, dst, to_band, to_sector).start()

        def send(step, carry):
            put(step, field_ref, lambda at: far_tgt_ref[section, at])
            return carry

        def pass_on(step, carry):
            put(step, passing, lambda at: targets[section, 0, at])
            return carry

        @pl.when(relays)
        def _():
            field_copy().start()
            if first:
                target_copy().start()

        lax.fori_loop(0, near_steps, send, 0)

        if first:
            lax.fori_loop(0, cells, send_codes, 0)

        if first:
            far_values[...] = jnp.zeros_like(far_values)

        def own_products(step, carry):
            for k in range(own_group):
                at = step * own_group + k
                code = own_ref[section, at]
                own_values[pl.ds(at, channels, stride=own), :] = product(
                    field_ref[code & MASK], tiles_ref[code >> SHIFT]
                )
            return carry

        lax.fori_loop(0, own // own_group, own_products, 0)

        block_ids = lax.broadcasted_iota(jnp.int32, (blocks, own), 0)
        own_pick = (block_ids == own_src_ref[section]).astype(jnp.float32).astype(jnp.bfloat16)

        def own_sum(c, carry):
            high, low = split(own_values[pl.ds(pl.multiple_of(c * own, 8), own), :])
            both = jnp.dot(
                own_pick,
                jnp.concatenate([high, low], 1),
                preferred_element_type=jnp.float32,
            )
            total[pl.ds(pl.multiple_of(c * blocks, 8), blocks), :] = (
                both[:, :points] + both[:, points:]
            )
            return carry

        lax.fori_loop(0, channels, own_sum, 0)

        @pl.when(jnp.logical_not(relays))
        def _():
            lax.fori_loop(near_steps, cells, send, 0)


        if first:
            lax.fori_loop(0, cells, wait_codes, 0)
            local = pltpu.make_async_copy(codes_in, codes, code_sem)
            local.start()
            local.wait()

        row_ids = lax.broadcasted_iota(jnp.int32, (pad, points), 0)
        lane_ids = lax.broadcasted_iota(jnp.int32, (pad, points), 1)

        def far_products(step, carry):
            dst, mine = in_cell(step)

            @pl.when(jnp.logical_not(mine))
            def _():
                data_copy(dst, dst, band, sector).wait_recv()

            wanted = jnp.full((pad, points), -1, jnp.int32)
            for k in range(cap):
                code = codes[dst, 0, turn * cap + k]
                far_values[pl.ds(step * pad + k, channels, stride=rows), :] = product(
                    recv[turn, dst, k], tiles_ref[code >> SHIFT]
                )
                wanted = jnp.where(row_ids == k, code & MASK, wanted)
            picks[pl.ds(pl.multiple_of(step * pad, pad), pad), :] = (wanted == lane_ids).astype(
                jnp.float32
            )
            return carry

        per_chunk = chunk // pad
        for part in range(rows // chunk):
            if part == 0:

                @pl.when(relays)
                def _():
                    if first:
                        target_copy().wait_recv()
                        listed = pltpu.make_async_copy(targets_in, targets, code_sem)
                        listed.start()
                        listed.wait()
                    field_copy().wait_recv()
                    lax.fori_loop(near_steps, cells, pass_on, 0)

            lax.fori_loop(part * per_chunk, (part + 1) * per_chunk, far_products, 0)
            pick = picks[part * chunk : (part + 1) * chunk, :].T[:blocks].astype(jnp.bfloat16)
            pick = jnp.concatenate([pick, pick], 1)

            def far_sum(pair, carry):
                parts = []
                for c in range(2):
                    at = pl.multiple_of((pair * 2 + c) * rows + part * chunk, 8)
                    parts.append(jnp.concatenate(split(far_values[pl.ds(at, chunk), :]), 0))
                both = jnp.dot(
                    pick, jnp.concatenate(parts, 1), preferred_element_type=jnp.float32
                )
                for c in range(2):
                    at = pl.multiple_of((pair * 2 + c) * blocks, 8)
                    total[pl.ds(at, blocks), :] += both[:, c * points : (c + 1) * points]
                return carry

            lax.fori_loop(0, channels // 2, far_sum, 0, unroll=4)

        def drain(step, carry):
            held, _, dst, to_band, to_sector, mine = out_cell(step)

            @pl.when(jnp.logical_not(mine))
            def _():
                data_copy(held, dst, to_band, to_sector).wait_send()

            return carry

        lax.fori_loop(0, cells, drain, 0)

        @pl.when(relays)
        def _():
            field_copy().wait_send()
            if first:
                target_copy().wait_send()

        if first:
            lax.fori_loop(0, cells, drain_codes, 0)

        def finish(step, carry):
            for k in range(8):
                n = step * 8 + k
                value = total[pl.ds(n, channels, stride=blocks), :]
                if first:
                    middle[n] = value.astype(jnp.bfloat16)
                else:
                    out_ref[n] = value
            return carry

        lax.fori_loop(0, blocks // 8, finish, 0)


def both_steps(bands, sectors, own_codes, targets, own_src, codes, field, tiles):
    far_tgt = targets[:, 0]
    cells = sectors * 3
    cap = far_tgt.shape[1] // cells
    pad = (cap + 15) // 16 * 16
    blocks, channels, points = field.shape
    own = own_codes.shape[1]
    smem = pl.BlockSpec(memory_space=pltpu.SMEM)
    vmem = pl.BlockSpec(memory_space=pltpu.VMEM)
    dma = pltpu.SemaphoreType.DMA
    entries = 2 * (own + far_tgt.shape[1])
    return pl.pallas_call(
        functools.partial(steps_kernel, bands, sectors),
        out_shape=jax.ShapeDtypeStruct(field.shape, jnp.float32),
        in_specs=[smem, smem, vmem, vmem, vmem, vmem, vmem],
        out_specs=vmem,
        scratch_shapes=[
            pltpu.VMEM(field.shape, jnp.bfloat16),
            pltpu.VMEM((cells, cap, channels, points), jnp.bfloat16),
            pltpu.VMEM((2, cells, cap, channels, points), jnp.bfloat16),
            pltpu.VMEM(codes.shape, jnp.int32),
            pltpu.SMEM(codes.shape, jnp.int32),
            pltpu.VMEM(field.shape, jnp.bfloat16),
            pltpu.VMEM(field.shape, jnp.bfloat16),
            pltpu.VMEM(targets.shape, jnp.int32),
            pltpu.SMEM(targets.shape, jnp.int32),
            pltpu.VMEM((channels * own, points), jnp.float32),
            pltpu.VMEM((channels * cells * pad, points), jnp.float32),
            pltpu.VMEM((cells * pad, points), jnp.float32),
            pltpu.VMEM((channels * blocks, points), jnp.float32),
            dma((2, cells)),
            dma((2, cells)),
            dma((cells,)),
            dma((cells,)),
            dma,
            dma((2,)),
            dma((2,)),
            dma,
            dma,
        ],
        compiler_params=pltpu.CompilerParams(
            collective_id=0, has_side_effects=True, vmem_limit_bytes=LIMIT
        ),
        cost_estimate=pl.CostEstimate(
            flops=2 * entries * channels * points * points,
            bytes_accessed=entries * channels * points * 8,
            transcendentals=0,
        ),
        name="both_steps",
    )(own_codes, far_tgt, own_src, codes, targets, field, tiles)


def on_device(
    bands,
    sectors,
    cotangent,
    tiles,
    local_src,
    local_tgt,
    local_tile,
    remote_src,
    remote_tgt,
    remote_tile,
    remote_live,
):
    field = cotangent[0]
    blocks = field.shape[0]
    cells = sectors * 3
    cap = remote_src.shape[2] // cells
    own_codes = local_tgt[:, 0] + (local_tile[:, 0] << SHIFT)
    source = jnp.where(remote_live[:, 0] > 0, remote_src[:, 0], blocks)
    far_codes = (source + (remote_tile[:, 0] << SHIFT)).reshape(2, cells, cap)
    codes = jnp.concatenate([far_codes[1], far_codes[0]], 1)
    codes = jnp.pad(codes, ((0, 0), (0, 128 - 2 * cap)))[:, None, :]
    summed = both_steps(
        bands, sectors, own_codes, remote_tgt, local_src, codes, field, tiles
    )
    return summed[None]


def solution(mesh):
    placed = (P("lat", "lon", None, None), P()) + (P(None, "lat", "lon"),) * 7
    return jax.shard_map(
        functools.partial(on_device, mesh.shape["lat"], mesh.shape["lon"]),
        mesh=mesh,
        in_specs=placed,
        out_specs=P("lat", "lon", None, None),
        check_vma=False,
    )
```
